32 devices in a mesh: groups: 2 (over y), mp: 4 (over x, core), hidden: 4 (over z).
Axes of the slice: x: 2, y: 2, z: 4, core: 2. Of those that a mesh axis runs over, the one named last changes fastest.
Arguments:
- tokens: bfloat16 [768, 8192], P(('groups', 'hidden'), 'mp'), parts along dimension 0, may hold values from -6 to 6
- block_mask: int32 [768, 64], P(('groups', 'hidden'), 'mp'), parts along dimension 0, may hold values from 0 to 1, as said below
- gate_weight: bfloat16 [8192, 26624], P('mp', 'hidden'), may hold values from -0.0625 to 0.0625
- up_weight: bfloat16 [8192, 26624], P('mp', 'hidden'), may hold values from -0.0625 to 0.0625
- down_weight: bfloat16 [26624, 8192], P('hidden', 'mp'), may hold values from -0.0390625 to 0.0390625
Outputs:
- mixed: bfloat16 [768, 8192], P(('groups', 'hidden'), 'mp'), parts along dimension 0
The draws below stay inside these ranges and needn't reach their ends.
There are 2 independent parts, one for each index of `groups`. The reference program is written for one: setup_inputs(seed, part) draws one part's arguments, and reference() takes and returns one part's arrays. A program takes and returns all parts, laid end to end along the dimension named above; an argument that names none is the same for every part. Nothing has to cross between parts.
Inputs may be any that keep to these rules, and one draw needn't show every extreme that they name: `block_mask`: each row has exactly 25 active blocks; some blocks are active in far more rows than others.
All inputs are finite; a program needn't handle non-finite values.
Results may differ from the reference program's by a relative error of at most 0.0051.
Values may be sent and summed in bfloat16 or wider, within the bound.
A program may use at most 256 MiB of HBM per device.

```python
import jax
import jax.numpy as jnp
from jax import lax

D = 8192
FF = 26624
BLOCK = 128
ROWS = 384
DB = 64
KB = 25


def draw_block_mask(key, part):
    key = jax.random.fold_in(key, 11)
    first, second = jax.random.split(key)
    favour = jax.random.randint(first, (DB,), 0, 3 * DB)
    jitter = jax.random.randint(second, (ROWS, DB), 0, 4 * DB)
    scores = (jitter + favour[None, :]) * DB + jnp.arange(DB, dtype=jnp.int32)[None, :]
    values, places = lax.top_k(scores, KB)
    cutoff = values[:, KB - 1:KB]
    return (scores >= cutoff).astype(jnp.int32)


def levels(key, dims, cuts, smallest, high):
    factor_of, own = 1.0, jax.random.fold_in(key, 6)
    for dim, blocks in cuts:
        draws = jnp.exp(jax.random.uniform(jax.random.fold_in(own, dim), (blocks,), jnp.float32, smallest / len(cuts), high / len(cuts)))
        factor_of = factor_of * jnp.repeat(draws, dims[dim] // blocks).reshape([-1 if axis == dim else 1 for axis in range(len(dims))])
    return factor_of


def scatter_about(own_key, dims, width, bound, shards=(), kind=jnp.bfloat16):
    gain = levels(own_key, dims, shards, -0.22, 0.18) if shards else 1.0
    entries = jax.random.normal(own_key, dims, jnp.float32) * width * gain
    return jnp.minimum(jnp.maximum(entries, -bound), bound).astype(kind)


def setup_inputs(seed: int = 0, part: int = 0) -> dict:
    splits = jax.random.split(jax.random.key(seed), 6)
    part_splits = jax.random.split(jax.random.fold_in(splits[5], part), 6)
    tokens = scatter_about(part_splits[0], (ROWS, D), 1.0, 6.0, ((0, 4), (1, 4)))
    block_mask = draw_block_mask(jax.random.fold_in(jax.random.fold_in(splits[5], part), 71), part)
    gate_weight = scatter_about(splits[2], (D, FF), D ** -0.5, 0.0625, ((0, 4), (1, 4)))
    up_weight = scatter_about(splits[3], (D, FF), D ** -0.5, 0.0625, ((0, 4), (1, 4)))
    down_weight = scatter_about(splits[4], (FF, D), FF ** -0.5, 0.0390625, ((0, 4), (1, 4)))
    return dict(tokens=tokens, block_mask=block_mask, gate_weight=gate_weight, up_weight=up_weight, down_weight=down_weight)


def reference(tokens, block_mask, gate_weight, up_weight, down_weight):
    keep = jnp.repeat(block_mask, BLOCK, axis=1).astype(jnp.bfloat16)
    masked = tokens * keep
    gate = jnp.dot(masked, gate_weight, preferred_element_type=jnp.float32)
    upward = jnp.dot(masked, up_weight, preferred_element_type=jnp.float32)
    hidden = (jax.nn.silu(gate) * upward).astype(jnp.bfloat16)
    return jnp.dot(hidden, down_weight, preferred_element_type=jnp.float32).astype(jnp.bfloat16)
```

```python
import jax
import jax.numpy as jnp
import numpy as np
from jax import lax
from jax.sharding import PartitionSpec as P

BLOCK = 128
CHUNKS = 5


def widths(units):
    step = 256
    tiles = units // step
    parts = min(CHUNKS, tiles)
    sizes = [(tiles // parts + (1 if i < tiles % parts else 0)) * step for i in range(parts)]
    sizes[-1] += units - sum(sizes)
    return sizes


def local(tokens, block_mask, gate_weight, up_weight, down_weight):
    n = lax.axis_size("mp")
    z = lax.axis_size("hidden")
    me = lax.axis_index("mp")
    mz = lax.axis_index("hidden")
    rows, features = tokens.shape
    cols = down_weight.shape[1]
    units = gate_weight.shape[1]
    r = rows // n
    bits = [1 << i for i in range(n.bit_length() - 1)]
    masks = np.array(
        [sum(b for l, b in enumerate(bits) if not (p >> (len(bits) - 1 - l)) & 1) for p in range(n)], np.int32
    )
    inverse = np.argsort(masks).astype(np.int32)

    def swap(x, bit):
        return lax.ppermute(x, "mp", [(i, i ^ bit) for i in range(n)])

    keep = jnp.repeat(block_mask, BLOCK, axis=1).astype(tokens.dtype)
    masked = (tokens * keep).reshape(n, r, features)
    masked = jnp.take(masked, me ^ jnp.asarray(masks), axis=0)
    all_rows = lax.all_gather(masked, "hidden", axis=1, tiled=True).reshape(n * z * r, features)

    acc = None
    start = 0
    for width in widths(units):
        stop = start + width
        gate = jnp.dot(all_rows, gate_weight[:, start:stop], preferred_element_type=jnp.float32)
        up = jnp.dot(all_rows, up_weight[:, start:stop], preferred_element_type=jnp.float32)
        for bit in bits:
            half = gate.shape[0] // 2
            sent = jnp.concatenate([gate[:half].astype(jnp.bfloat16), up[:half].astype(jnp.bfloat16)], axis=0)
            got = swap(sent, bit)
            gate = gate[half:] + got[:half].astype(jnp.float32)
            up = up[half:] + got[half:].astype(jnp.float32)
        hidden = (jax.nn.silu(gate) * up).astype(jnp.bfloat16)
        for bit in reversed(bits):
            hidden = jnp.concatenate([swap(hidden, bit), hidden], axis=0)
        part = jnp.dot(hidden, down_weight[start:stop], preferred_element_type=jnp.float32)
        acc = part if acc is None else acc + part
        start = stop

    acc = acc.reshape(n, z, r, cols)
    total = lax.dynamic_index_in_dim(acc, mz, 1, keepdims=False)
    for s in range(1, z):
        block = lax.dynamic_index_in_dim(acc, (mz + s) % z, 1, keepdims=False).astype(jnp.bfloat16)
        got = lax.ppermute(block, "hidden", [(i, (i + s) % z) for i in range(z)])
        total = total + got.astype(jnp.float32)
    total = jnp.take(total.astype(jnp.bfloat16), jnp.asarray(inverse)[me ^ jnp.arange(n)], axis=0)
    return total.reshape(rows, cols)


def solution(mesh):
    in_specs = (
        P(("groups", "hidden"), "mp"),
        P(("groups", "hidden"), "mp"),
        P("mp", "hidden"),
        P("mp", "hidden"),
        P("hidden", "mp"),
    )
    out_specs = P(("groups", "hidden"), "mp")
    return jax.shard_map(local, mesh=mesh, in_specs=in_specs, out_specs=out_specs, check_vma=False)
```

```python
import functools

import jax
import jax.numpy as jnp
import numpy as np
from jax import lax
from jax.experimental import pallas as pl
from jax.experimental.pallas import tpu as pltpu
from jax.sharding import PartitionSpec as P

BLOCK = 128
CHUNKS = 5


def widths(units):
    step = 256
    tiles = units // step
    parts = min(CHUNKS, tiles)
    sizes = [(tiles // parts + (1 if i < tiles % parts else 0)) * step for i in range(parts)]
    sizes[-1] += units - sum(sizes)
    return sizes


PASSES = 2
WIDTH = 512
LAG_ACT, LAG_FWD, LAG_DOWN = 3, 6, 7
WSLOTS = 3
KSLOTS = 4


def fused_kernel(z, n_iter, per_pass, tokens, keep, wg, wu, wd, out,
                 rows_buf, wg_buf, wu_buf, wd_buf, held, core_out, core_in, x_out, x_in, hid, acc, z_out, z_in,
                 wg_sem, wu_sem, wd_sem, ag_s, ag_r, core_s, core_r, x_s, x_r, hx_s, hx_r, hc_s, hc_r, z_s, z_r):
    f32, bf16 = jnp.float32, jnp.bfloat16
    me = lax.axis_index("mp")
    mz = lax.axis_index("hidden")
    k, xb = me % 2, me // 2
    core_peer = xb * 2 + (1 - k)
    x_peer = (1 - xb) * 2 + k
    b = rows_buf.shape[2]
    w = WIDTH
    mesh_id = pl.DeviceIdType.MESH

    def place(j):
        return ((j // 2 + 1 - k) % 2) * 2 + (j + 1 - xb) % 2

    def wg_copy(i):
        c = i % per_pass
        return pltpu.make_async_copy(wg.at[:, pl.ds(pl.multiple_of(c * w, w), w)], wg_buf.at[i % WSLOTS], wg_sem.at[i % WSLOTS])

    def wu_copy(i):
        c = i % per_pass
        return pltpu.make_async_copy(wu.at[:, pl.ds(pl.multiple_of(c * w, w), w)], wu_buf.at[i % WSLOTS], wu_sem.at[i % WSLOTS])

    def wd_copy(i):
        c = i % per_pass
        return pltpu.make_async_copy(wd.at[pl.ds(pl.multiple_of(c * w, w), w), :], wd_buf.at[i % WSLOTS], wd_sem.at[i % WSLOTS])

    def remote(src, dst, s, r, device):
        return pltpu.make_async_remote_copy(src_ref=src, dst_ref=dst, send_sem=s, recv_sem=r, device_id=device, device_id_type=mesh_id)

    def ag_copy(q, s):
        here = rows_buf.at[q, place(mz)]
        return remote(here, here, ag_s.at[q, s - 1], ag_r.at[q, s - 1], {"hidden": (mz + s) % z})

    def core_copy(i):
        return remote(core_out.at[i], core_in.at[i], core_s.at[i], core_r.at[i], {"mp": core_peer})

    def x_copy(i):
        return remote(x_out.at[i], x_in.at[i], x_s.at[i], x_r.at[i], {"mp": x_peer})

    def hx_copy(i):
        return remote(hid.at[i, pl.ds(3 * b, b)], hid.at[i, pl.ds(2 * b, b)], hx_s.at[i], hx_r.at[i], {"mp": x_peer})

    def hc_copy(i):
        return remote(hid.at[i, pl.ds(2 * b, 2 * b)], hid.at[i, pl.ds(0, 2 * b)], hc_s.at[i], hc_r.at[i], {"mp": core_peer})

    def z_copy(q, s):
        return remote(z_out.at[q, s - 1], z_in.at[q, s - 1], z_s.at[q, s - 1], z_r.at[q, s - 1], {"hidden": (mz + s) % z})

    for i in range(min(WSLOTS, n_iter)):
        wg_copy(i).start()
        wu_copy(i).start()
    for i in range(min(WSLOTS, n_iter)):
        wd_copy(i).start()

    barrier = pltpu.get_barrier_semaphore()
    pl.semaphore_signal(barrier, inc=1, device_id={"mp": core_peer}, device_id_type=mesh_id)
    pl.semaphore_signal(barrier, inc=1, device_id={"mp": x_peer}, device_id_type=mesh_id)
    for s in range(1, z):
        pl.semaphore_signal(barrier, inc=1, device_id={"hidden": (mz + s) % z}, device_id_type=mesh_id)

    mine = place(mz)
    for q in range(PASSES):
        for j in range(keep.shape[1]):
            piece = tokens[q * b:(q + 1) * b, j * BLOCK:(j + 1) * BLOCK].astype(f32)
            factor = keep[q * b:(q + 1) * b, j:j + 1].astype(f32)
            rows_buf[q, mine, :, j * BLOCK:(j + 1) * BLOCK] = (piece * factor).astype(bf16)

    pl.semaphore_wait(barrier, 2 + z - 1)
    for q in range(PASSES):
        for s in range(1, z):
            ag_copy(q, s).start()

    def project(i):
        q = i // per_pass

        @pl.when(i % per_pass == 0)
        def _():
            for s in range(1, z):
                ag_copy(q, s).wait_recv()

        rows = rows_buf[q].reshape(4 * b, rows_buf.shape[3])
        wg_copy(i).wait()
        slot = i % WSLOTS
        gate = jnp.dot(rows, wg_buf[slot], preferred_element_type=f32)
        core_out[i, :, 0:w] = gate[:2 * b].astype(bf16)
        held[i % KSLOTS, :, 0:w] = gate[2 * b:]
        wu_copy(i).wait()
        up = jnp.dot(rows, wu_buf[slot], preferred_element_type=f32)
        core_out[i, :, w:2 * w] = up[:2 * b].astype(bf16)
        core_copy(i).start()
        held[i % KSLOTS, :, w:2 * w] = up[2 * b:]

        @pl.when(i + WSLOTS < n_iter)
        def _():
            wg_copy(i + WSLOTS).start()
            wu_copy(i + WSLOTS).start()

    def combine(i):
        core_copy(i).wait_recv()
        slot = i % KSLOTS
        x_out[i] = (held[slot, 0:b] + core_in[i, 0:b].astype(f32)).astype(bf16)
        x_copy(i).start()
        held[slot, b:2 * b] = held[slot, b:2 * b] + core_in[i, b:2 * b].astype(f32)

    def act(i):
        x_copy(i).wait_recv()
        slot = i % KSLOTS
        gate = held[slot, b:2 * b, 0:w] + x_in[i, :, 0:w].astype(f32)
        up = held[slot, b:2 * b, w:2 * w] + x_in[i, :, w:2 * w].astype(f32)
        hid[i, 3 * b:4 * b] = (gate / (1.0 + jnp.exp(-gate)) * up).astype(bf16)
        hx_copy(i).start()

    def forward(i):
        hx_copy(i).wait_recv()
        hc_copy(i).start()

    def down(i):
        q = i // per_pass
        hc_copy(i).wait_recv()
        wd_copy(i).wait()
        part = jnp.dot(hid[i], wd_buf[i % WSLOTS], preferred_element_type=f32).reshape(4, b, acc.shape[3])

        @pl.when(i % per_pass == 0)
        def _():
            acc[q] = part

        @pl.when(i % per_pass != 0)
        def _():
            acc[q] = acc[q] + part

        @pl.when(i + WSLOTS < n_iter)
        def _():
            wd_copy(i + WSLOTS).start()

        @pl.when(i % per_pass == per_pass - 1)
        def _():
            for s in range(1, z):
                z_out[q, s - 1] = acc[q, place((mz + s) % z)].astype(bf16)
                z_copy(q, s).start()

    def step(t, carry):
        for stage, lag in ((project, 0), (combine, 1), (act, LAG_ACT), (forward, LAG_FWD), (down, LAG_DOWN)):
            @pl.when(jnp.logical_and(t >= lag, t < n_iter + lag))
            def _(stage=stage, lag=lag):
                stage(t - lag)
        return carry

    lax.fori_loop(0, n_iter + LAG_DOWN, step, 0)

    def drain(i, carry):
        core_copy(i).wait_send()
        x_copy(i).wait_send()
        hx_copy(i).wait_send()
        hc_copy(i).wait_send()
        return carry

    lax.fori_loop(0, n_iter, drain, 0)
    for q in range(PASSES):
        total = acc[q, mine]
        for s in range(1, z):
            ag_copy(q, s).wait_send()
            z_copy(q, s).wait()
            total = total + z_in[q, s - 1].astype(f32)
        out[q * b:(q + 1) * b, :] = total.astype(bf16)


def fused(tokens, block_mask, gate_weight, up_weight, down_weight):
    z = lax.axis_size("hidden")
    rows, features = tokens.shape
    units = gate_weight.shape[1]
    cols = down_weight.shape[1]
    b = rows // PASSES
    per_pass = units // WIDTH
    n = per_pass * PASSES
    f32, bf16 = jnp.float32, jnp.bfloat16
    dma = pltpu.SemaphoreType.DMA
    flops = 2 * rows * z * units * (2 * features + cols)
    vmem = pl.BlockSpec(memory_space=pltpu.VMEM)
    hbm = pl.BlockSpec(memory_space=pl.ANY)
    return pl.pallas_call(
        functools.partial(fused_kernel, z, n, per_pass),
        out_shape=jax.ShapeDtypeStruct((rows, cols), bf16),
        in_specs=[vmem, vmem, hbm, hbm, hbm],
        out_specs=vmem,
        scratch_shapes=[
            pltpu.VMEM((PASSES, z, b, features), bf16),
            pltpu.VMEM((WSLOTS, features, WIDTH), bf16),
            pltpu.VMEM((WSLOTS, features, WIDTH), bf16),
            pltpu.VMEM((WSLOTS, WIDTH, cols), bf16),
            pltpu.VMEM((KSLOTS, 2 * b, 2 * WIDTH), f32),
            pltpu.VMEM((n, 2 * b, 2 * WIDTH), bf16),
            pltpu.VMEM((n, 2 * b, 2 * WIDTH), bf16),
            pltpu.VMEM((n, b, 2 * WIDTH), bf16),
            pltpu.VMEM((n, b, 2 * WIDTH), bf16),
            pltpu.VMEM((n, 4 * b, WIDTH), bf16),
            pltpu.VMEM((PASSES, z, b, cols), f32),
            pltpu.VMEM((PASSES, z - 1, b, cols), bf16),
            pltpu.VMEM((PASSES, z - 1, b, cols), bf16),
            dma((WSLOTS,)), dma((WSLOTS,)), dma((WSLOTS,)),
            dma((PASSES, z - 1)), dma((PASSES, z - 1)),
            dma((n,)), dma((n,)), dma((n,)), dma((n,)), dma((n,)), dma((n,)), dma((n,)), dma((n,)),
            dma((PASSES, z - 1)), dma((PASSES, z - 1)),
        ],
        compiler_params=pltpu.CompilerParams(
            collective_id=0, has_side_effects=True, vmem_limit_bytes=60 * 1024 * 1024
        ),
        cost_estimate=pl.CostEstimate(
            flops=flops, bytes_accessed=2 * PASSES * units * (2 * features + cols), transcendentals=rows * z * units
        ),
    )(tokens, block_mask, gate_weight, up_weight, down_weight)


def local(tokens, block_mask, gate_weight, up_weight, down_weight):
    n = lax.axis_size("mp")
    z = lax.axis_size("hidden")
    me = lax.axis_index("mp")
    mz = lax.axis_index("hidden")
    rows, features = tokens.shape
    cols = down_weight.shape[1]
    units = gate_weight.shape[1]
    if n == 4 and z == 4 and units % WIDTH == 0 and rows % (16 * PASSES) == 0:
        return fused(tokens, block_mask, gate_weight, up_weight, down_weight)
    r = rows // n
    bits = [1 << i for i in range(n.bit_length() - 1)]
    masks = np.array(
        [sum(b for l, b in enumerate(bits) if not (p >> (len(bits) - 1 - l)) & 1) for p in range(n)], np.int32
    )
    inverse = np.argsort(masks).astype(np.int32)

    def swap(x, bit):
        return lax.ppermute(x, "mp", [(i, i ^ bit) for i in range(n)])

    keep = jnp.repeat(block_mask, BLOCK, axis=1).astype(tokens.dtype)
    masked = (tokens * keep).reshape(n, r, features)
    masked = jnp.take(masked, me ^ jnp.asarray(masks), axis=0)
    all_rows = lax.all_gather(masked, "hidden", axis=1, tiled=True).reshape(n * z * r, features)

    acc = None
    start = 0
    for width in widths(units):
        stop = start + width
        gate = jnp.dot(all_rows, gate_weight[:, start:stop], preferred_element_type=jnp.float32)
        up = jnp.dot(all_rows, up_weight[:, start:stop], preferred_element_type=jnp.float32)
        for bit in bits:
            half = gate.shape[0] // 2
            sent = jnp.concatenate([gate[:half].astype(jnp.bfloat16), up[:half].astype(jnp.bfloat16)], axis=0)
            got = swap(sent, bit)
            gate = gate[half:] + got[:half].astype(jnp.float32)
            up = up[half:] + got[half:].astype(jnp.float32)
        hidden = (jax.nn.silu(gate) * up).astype(jnp.bfloat16)
        for bit in reversed(bits):
            hidden = jnp.concatenate([swap(hidden, bit), hidden], axis=0)
        part = jnp.dot(hidden, down_weight[start:stop], preferred_element_type=jnp.float32)
        acc = part if acc is None else acc + part
        start = stop

    acc = acc.reshape(n, z, r, cols)
    total = lax.dynamic_index_in_dim(acc, mz, 1, keepdims=False)
    for s in range(1, z):
        block = lax.dynamic_index_in_dim(acc, (mz + s) % z, 1, keepdims=False).astype(jnp.bfloat16)
        got = lax.ppermute(block, "hidden", [(i, (i + s) % z) for i in range(z)])
        total = total + got.astype(jnp.float32)
    total = jnp.take(total.astype(jnp.bfloat16), jnp.asarray(inverse)[me ^ jnp.arange(n)], axis=0)
    return total.reshape(rows, cols)


def solution(mesh):
    in_specs = (
        P(("groups", "hidden"), "mp"),
        P(("groups", "hidden"), "mp"),
        P("mp", "hidden"),
        P("mp", "hidden"),
        P("hidden", "mp"),
    )
    out_specs = P(("groups", "hidden"), "mp")
    return jax.shard_map(local, mesh=mesh, in_specs=in_specs, out_specs=out_specs, check_vma=False)
```

```python
import functools

import jax
import jax.numpy as jnp
import numpy as np
from jax import lax
from jax.experimental import pallas as pl
from jax.experimental.pallas import tpu as pltpu
from jax.sharding import PartitionSpec as P

BLOCK = 128
CHUNKS = 5


def widths(units):
    step = 256
    tiles = units // step
    parts = min(CHUNKS, tiles)
    sizes = [(tiles // parts + (1 if i < tiles % parts else 0)) * step for i in range(parts)]
    sizes[-1] += units - sum(sizes)
    return sizes


PASSES = 3
WIDTH = 512
LAG_ACT, LAG_FWD, LAG_DOWN = 3, 6, 7
WSLOTS = 3
KSLOTS = 4


def fused_kernel(z, n_iter, per_pass, tokens, keep, wg, wu, wd, out,
                 rows_buf, wg_buf, wu_buf, wd_buf, held, core_out, core_in, x_out, x_in, hid, acc, z_out, z_in,
                 wg_sem, wu_sem, wd_sem, ag_s, ag_r, core_s, core_r, x_s, x_r, hx_s, hx_r, hc_s, hc_r, z_s, z_r):
    f32, bf16 = jnp.float32, jnp.bfloat16
    me = lax.axis_index("mp")
    mz = lax.axis_index("hidden")
    k, xb = me % 2, me // 2
    core_peer = xb * 2 + (1 - k)
    x_peer = (1 - xb) * 2 + k
    b = rows_buf.shape[2]
    w = WIDTH
    mesh_id = pl.DeviceIdType.MESH

    def place(j):
        return ((j // 2 + 1 - k) % 2) * 2 + (j + 1 - xb) % 2

    def wg_copy(i):
        c = i % per_pass
        return pltpu.make_async_copy(wg.at[:, pl.ds(pl.multiple_of(c * w, w), w)], wg_buf.at[i % WSLOTS], wg_sem.at[i % WSLOTS])

    def wu_copy(i):
        c = i % per_pass
        return pltpu.make_async_copy(wu.at[:, pl.ds(pl.multiple_of(c * w, w), w)], wu_buf.at[i % WSLOTS], wu_sem.at[i % WSLOTS])

    def wd_copy(i):
        c = i % per_pass
        return pltpu.make_async_copy(wd.at[pl.ds(pl.multiple_of(c * w, w), w), :], wd_buf.at[i % WSLOTS], wd_sem.at[i % WSLOTS])

    def remote(src, dst, s, r, device):
        return pltpu.make_async_remote_copy(src_ref=src, dst_ref=dst, send_sem=s, recv_sem=r, device_id=device, device_id_type=mesh_id)

    def ag_copy(q, s):
        here = rows_buf.at[q, place(mz)]
        return remote(here, here, ag_s.at[q, s - 1], ag_r.at[q, s - 1], {"hidden": (mz + s) % z})

    def core_copy(i):
        return remote(core_out.at[i], core_in.at[i], core_s.at[i], core_r.at[i], {"mp": core_peer})

    def x_copy(i):
        return remote(x_out.at[i], x_in.at[i], x_s.at[i], x_r.at[i], {"mp": x_peer})

    def hx_copy(i):
        return remote(hid.at[i, pl.ds(3 * b, b)], hid.at[i, pl.ds(2 * b, b)], hx_s.at[i], hx_r.at[i], {"mp": x_peer})

    def hc_copy(i):
        return remote(hid.at[i, pl.ds(2 * b, 2 * b)], hid.at[i, pl.ds(0, 2 * b)], hc_s.at[i], hc_r.at[i], {"mp": core_peer})

    def z_copy(q, s):
        return remote(z_out.at[q, s - 1], z_in.at[q, s - 1], z_s.at[q, s - 1], z_r.at[q, s - 1], {"hidden": (mz + s) % z})

    for i in range(min(WSLOTS, n_iter)):
        wg_copy(i).start()
        wu_copy(i).start()
    for i in range(min(WSLOTS, n_iter)):
        wd_copy(i).start()

    barrier = pltpu.get_barrier_semaphore()
    pl.semaphore_signal(barrier, inc=1, device_id={"mp": core_peer}, device_id_type=mesh_id)
    pl.semaphore_signal(barrier, inc=1, device_id={"mp": x_peer}, device_id_type=mesh_id)
    for s in range(1, z):
        pl.semaphore_signal(barrier, inc=1, device_id={"hidden": (mz + s) % z}, device_id_type=mesh_id)

    mine = place(mz)
    for q in range(PASSES):
        for j in range(keep.shape[1]):
            piece = tokens[q * b:(q + 1) * b, j * BLOCK:(j + 1) * BLOCK].astype(f32)
            factor = keep[q * b:(q + 1) * b, j:j + 1].astype(f32)
            rows_buf[q, mine, :, j * BLOCK:(j + 1) * BLOCK] = (piece * factor).astype(bf16)

    pl.semaphore_wait(barrier, 2 + z - 1)
    for s in range(1, z):
        ag_copy(0, s).start()

    def project(i):
        q = i // per_pass

        @pl.when(i % per_pass == 0)
        def _():
            for s in range(1, z):
                ag_copy(q, s).wait_recv()

            @pl.when(q + 1 < PASSES)
            def _():
                for s in range(1, z):
                    ag_copy(q + 1, s).start()

        rows = rows_buf[q].reshape(4 * b, rows_buf.shape[3])
        wg_copy(i).wait()
        slot = i % WSLOTS
        gate = jnp.dot(rows, wg_buf[slot], preferred_element_type=f32)
        core_out[i, :, 0:w] = gate[:2 * b].astype(bf16)
        held[i % KSLOTS, :, 0:w] = gate[2 * b:]
        wu_copy(i).wait()
        up = jnp.dot(rows, wu_buf[slot], preferred_element_type=f32)
        core_out[i, :, w:2 * w] = up[:2 * b].astype(bf16)
        core_copy(i).start()
        held[i % KSLOTS, :, w:2 * w] = up[2 * b:]

        @pl.when(i + WSLOTS < n_iter)
        def _():
            wg_copy(i + WSLOTS).start()
            wu_copy(i + WSLOTS).start()

    def combine(i):
        core_copy(i).wait_recv()
        slot = i % KSLOTS
        x_out[i] = (held[slot, 0:b] + core_in[i, 0:b].astype(f32)).astype(bf16)
        x_copy(i).start()
        held[slot, b:2 * b] = held[slot, b:2 * b] + core_in[i, b:2 * b].astype(f32)

    def act(i):
        x_copy(i).wait_recv()
        slot = i % KSLOTS
        gate = held[slot, b:2 * b, 0:w] + x_in[i, :, 0:w].astype(f32)
        up = held[slot, b:2 * b, w:2 * w] + x_in[i, :, w:2 * w].astype(f32)
        hid[i, 3 * b:4 * b] = (gate / (1.0 + jnp.exp(-gate)) * up).astype(bf16)
        hx_copy(i).start()

    def forward(i):
        hx_copy(i).wait_recv()
        hc_copy(i).start()

    def down(i):
        q = i // per_pass
        hc_copy(i).wait_recv()
        wd_copy(i).wait()
        part = jnp.dot(hid[i], wd_buf[i % WSLOTS], preferred_element_type=f32).reshape(4, b, acc.shape[3])

        @pl.when(i % per_pass == 0)
        def _():
            acc[q] = part

        @pl.when(i % per_pass != 0)
        def _():
            acc[q] = acc[q] + part

        @pl.when(i + WSLOTS < n_iter)
        def _():
            wd_copy(i + WSLOTS).start()

        @pl.when(i % per_pass == per_pass - 1)
        def _():
            for s in range(1, z):
                z_out[q, s - 1] = acc[q, place((mz + s) % z)].astype(bf16)
                z_copy(q, s).start()

    def step(t, carry):
        for stage, lag in ((project, 0), (combine, 1), (act, LAG_ACT), (forward, LAG_FWD), (down, LAG_DOWN)):
            @pl.when(jnp.logical_and(t >= lag, t < n_iter + lag))
            def _(stage=stage, lag=lag):
                stage(t - lag)
        return carry

    lax.fori_loop(0, n_iter + LAG_DOWN, step, 0)

    def drain(i, carry):
        core_copy(i).wait_send()
        x_copy(i).wait_send()
        hx_copy(i).wait_send()
        hc_copy(i).wait_send()
        return carry

    lax.fori_loop(0, n_iter, drain, 0)
    for q in range(PASSES):
        total = acc[q, mine]
        for s in range(1, z):
            ag_copy(q, s).wait_send()
            z_copy(q, s).wait()
            total = total + z_in[q, s - 1].astype(f32)
        out[q * b:(q + 1) * b, :] = total.astype(bf16)


def fused(tokens, block_mask, gate_weight, up_weight, down_weight):
    z = lax.axis_size("hidden")
    rows, features = tokens.shape
    units = gate_weight.shape[1]
    cols = down_weight.shape[1]
    b = rows // PASSES
    per_pass = units // WIDTH
    n = per_pass * PASSES
    f32, bf16 = jnp.float32, jnp.bfloat16
    dma = pltpu.SemaphoreType.DMA
    flops = 2 * rows * z * units * (2 * features + cols)
    vmem = pl.BlockSpec(memory_space=pltpu.VMEM)
    hbm = pl.BlockSpec(memory_space=pl.ANY)
    return pl.pallas_call(
        functools.partial(fused_kernel, z, n, per_pass),
        out_shape=jax.ShapeDtypeStruct((rows, cols), bf16),
        in_specs=[vmem, vmem, hbm, hbm, hbm],
        out_specs=vmem,
        scratch_shapes=[
            pltpu.VMEM((PASSES, z, b, features), bf16),
            pltpu.VMEM((WSLOTS, features, WIDTH), bf16),
            pltpu.VMEM((WSLOTS, features, WIDTH), bf16),
            pltpu.VMEM((WSLOTS, WIDTH, cols), bf16),
            pltpu.VMEM((KSLOTS, 2 * b, 2 * WIDTH), f32),
            pltpu.VMEM((n, 2 * b, 2 * WIDTH), bf16),
            pltpu.VMEM((n, 2 * b, 2 * WIDTH), bf16),
            pltpu.VMEM((n, b, 2 * WIDTH), bf16),
            pltpu.VMEM((n, b, 2 * WIDTH), bf16),
            pltpu.VMEM((n, 4 * b, WIDTH), bf16),
            pltpu.VMEM((PASSES, z, b, cols), f32),
            pltpu.VMEM((PASSES, z - 1, b, cols), bf16),
            pltpu.VMEM((PASSES, z - 1, b, cols), bf16),
            dma((WSLOTS,)), dma((WSLOTS,)), dma((WSLOTS,)),
            dma((PASSES, z - 1)), dma((PASSES, z - 1)),
            dma((n,)), dma((n,)), dma((n,)), dma((n,)), dma((n,)), dma((n,)), dma((n,)), dma((n,)),
            dma((PASSES, z - 1)), dma((PASSES, z - 1)),
        ],
        compiler_params=pltpu.CompilerParams(
            collective_id=0, has_side_effects=True, vmem_limit_bytes=60 * 1024 * 1024
        ),
        cost_estimate=pl.CostEstimate(
            flops=flops, bytes_accessed=2 * PASSES * units * (2 * features + cols), transcendentals=rows * z * units
        ),
    )(tokens, block_mask, gate_weight, up_weight, down_weight)


def local(tokens, block_mask, gate_weight, up_weight, down_weight):
    n = lax.axis_size("mp")
    z = lax.axis_size("hidden")
    me = lax.axis_index("mp")
    mz = lax.axis_index("hidden")
    rows, features = tokens.shape
    cols = down_weight.shape[1]
    units = gate_weight.shape[1]
    if n == 4 and z == 4 and units % WIDTH == 0 and rows % (16 * PASSES) == 0:
        return fused(tokens, block_mask, gate_weight, up_weight, down_weight)
    r = rows // n
    bits = [1 << i for i in range(n.bit_length() - 1)]
    masks = np.array(
        [sum(b for l, b in enumerate(bits) if not (p >> (len(bits) - 1 - l)) & 1) for p in range(n)], np.int32
    )
    inverse = np.argsort(masks).astype(np.int32)

    def swap(x, bit):
        return lax.ppermute(x, "mp", [(i, i ^ bit) for i in range(n)])

    keep = jnp.repeat(block_mask, BLOCK, axis=1).astype(tokens.dtype)
    masked = (tokens * keep).reshape(n, r, features)
    masked = jnp.take(masked, me ^ jnp.asarray(masks), axis=0)
    all_rows = lax.all_gather(masked, "hidden", axis=1, tiled=True).reshape(n * z * r, features)

    acc = None
    start = 0
    for width in widths(units):
        stop = start + width
        gate = jnp.dot(all_rows, gate_weight[:, start:stop], preferred_element_type=jnp.float32)
        up = jnp.dot(all_rows, up_weight[:, start:stop], preferred_element_type=jnp.float32)
        for bit in bits:
            half = gate.shape[0] // 2
            sent = jnp.concatenate([gate[:half].astype(jnp.bfloat16), up[:half].astype(jnp.bfloat16)], axis=0)
            got = swap(sent, bit)
            gate = gate[half:] + got[:half].astype(jnp.float32)
            up = up[half:] + got[half:].astype(jnp.float32)
        hidden = (jax.nn.silu(gate) * up).astype(jnp.bfloat16)
        for bit in reversed(bits):
            hidden = jnp.concatenate([swap(hidden, bit), hidden], axis=0)
        part = jnp.dot(hidden, down_weight[start:stop], preferred_element_type=jnp.float32)
        acc = part if acc is None else acc + part
        start = stop

    acc = acc.reshape(n, z, r, cols)
    total = lax.dynamic_index_in_dim(acc, mz, 1, keepdims=False)
    for s in range(1, z):
        block = lax.dynamic_index_in_dim(acc, (mz + s) % z, 1, keepdims=False).astype(jnp.bfloat16)
        got = lax.ppermute(block, "hidden", [(i, (i + s) % z) for i in range(z)])
        total = total + got.astype(jnp.float32)
    total = jnp.take(total.astype(jnp.bfloat16), jnp.asarray(inverse)[me ^ jnp.arange(n)], axis=0)
    return total.reshape(rows, cols)


def solution(mesh):
    in_specs = (
        P(("groups", "hidden"), "mp"),
        P(("groups", "hidden"), "mp"),
        P("mp", "hidden"),
        P("mp", "hidden"),
        P("hidden", "mp"),
    )
    out_specs = P(("groups", "hidden"), "mp")
    return jax.shard_map(local, mesh=mesh, in_specs=in_specs, out_specs=out_specs, check_vma=False)
```
